512 devices in a mesh: row: 16 (over y, x_lo, core), col: 32 (over x_hi, z).
Axes of the slice: x: 4 (x_hi: 2, x_lo: 2; x = x_hi * 2 + x_lo), y: 4, z: 16, core: 2. Of those that a mesh axis runs over, the one named last changes fastest.
Arguments:
- features: bfloat16 [32768, 512], P(('col', 'row')), may hold values from -6 to 6
- positions: float32 [3, 32768], replicated, may hold values from 0 to 80, as said below
- cluster_atoms: int32 [256], replicated, may hold values from 64 to 128, as said below
- pair_cells: int32 [16, 32, 12], P('row', 'col'), may hold values from 0 to 127, as said below
- pair_count: int32 [16, 32], P('row', 'col'), may hold values from 1 to 12, as said below
- project_weight: bfloat16 [512, 512], replicated, may hold values from -0.25 to 0.25
- basis_filter: float32 [16, 512], replicated, may hold values from -0.375 to 0.375
- hidden_weight: bfloat16 [512, 512], replicated, may hold values from -0.25 to 0.25
- hidden_bias: float32 [512], replicated, may hold values from -4 to 4
- output_weight: bfloat16 [512, 512], replicated, may hold values from -0.25 to 0.25
- output_bias: float32 [512], replicated, may hold values from -3 to 3
Outputs:
- update: bfloat16 [32768, 512], P('row')
The draws below stay inside these ranges and needn't reach their ends.
Inputs may be any that keep to these rules, and one draw needn't show every extreme that they name: `positions`: each cluster's atoms lie in a cube of side 5 of its own. `cluster_atoms`: atoms of a cluster at slots below the count are real, the others padding; some cluster is full. `pair_cells`: entry v names target cluster v // 8 of the row's block of 16 clusters and source cluster v mod 8 of the column's block of 8 clusters; the entries of one device are distinct; only the first pair_count entries are used. `pair_count`: some device lists 12 pairs.
All inputs are finite; a program needn't handle non-finite values.
Results may differ from the reference program's by a relative error of at most 0.0048.
Values may be sent and summed in bfloat16 or wider, within the bound.
A program may use at most 64 MiB of HBM per device.

```python
import math
import jax
import jax.numpy as jnp
from jax import lax

CL = 128
F = 512
NRBF = 16
CPR = 16
PCAP = 12
SPC = 8
NCLUS = 256
NATOM = 32768
N_ROW = 16
N_COL = 32


cell_side = 5.0


def cluster_layout(key):
    order = jax.random.permutation(jax.random.fold_in(key, 5), NCLUS).astype(jnp.int32)
    cell_x = order % 4
    cell_y = order // 4 % 4
    cell_z = order // 16
    return jnp.stack([cell_x, cell_y, cell_z]).astype(jnp.int32)


def pair_layout(key):
    cells = cluster_layout(key)
    candidates = CPR * SPC
    rows = jnp.arange(N_ROW, dtype=jnp.int32)[:, None, None]
    cols = jnp.arange(N_COL, dtype=jnp.int32)[None, :, None]
    entries = jnp.arange(candidates, dtype=jnp.int32)[None, None, :]
    target = rows * CPR + entries // SPC
    source = cols * SPC + entries % SPC
    target = jnp.broadcast_to(target, (N_ROW, N_COL, candidates))
    source = jnp.broadcast_to(source, (N_ROW, N_COL, candidates))
    gap = jnp.max(jnp.abs(cells[:, target] - cells[:, source]), axis=0)
    nearness = jnp.minimum(gap, 2)
    device_keys = jax.random.split(jax.random.fold_in(key, 23), N_ROW * N_COL)
    ties = jax.vmap(lambda single: jax.random.permutation(single, candidates))(device_keys)
    ties = ties.reshape(N_ROW, N_COL, candidates).astype(jnp.int32)
    score = nearness * candidates + ties
    ranked = jnp.argsort(score, axis=-1, stable=True).astype(jnp.int32)
    listed_cells = ranked[:, :, :PCAP]
    adjacent = jnp.sum((gap <= 1).astype(jnp.int32), axis=-1)
    listed = jnp.clip(adjacent, 1, PCAP).reshape(-1)
    chosen = jax.random.randint(jax.random.fold_in(key, 37), (), 0, N_ROW * N_COL)
    listed = jnp.where(jnp.arange(N_ROW * N_COL) == chosen, PCAP, listed)
    return (listed_cells.astype(jnp.int32), listed.reshape(N_ROW, N_COL).astype(jnp.int32))


def draw_positions(key, part):
    cells = cluster_layout(key).astype(jnp.float32) * cell_side
    corners = jnp.repeat(cells, CL, axis=1)
    inside = jax.random.uniform(jax.random.fold_in(key, 7), (3, NATOM), jnp.float32, 0.0, cell_side)
    return (corners + inside).astype(jnp.float32)


def draw_cluster_atoms(key, part):
    count_key, pick_key = jax.random.split(jax.random.fold_in(key, 11))
    counts = jax.random.randint(count_key, (NCLUS,), CL // 2, CL + 1)
    chosen = jax.random.randint(pick_key, (), 0, NCLUS)
    return jnp.where(jnp.arange(NCLUS) == chosen, CL, counts).astype(jnp.int32)


def draw_pair_cells(key, part):
    return pair_layout(key)[0]


def draw_pair_count(key, part):
    return pair_layout(key)[1]


def block_levels(own_key, dims, cuts, smallest, largest):
    loudness = 1.0
    for position, parts in cuts:
        steps = jax.random.uniform(jax.random.fold_in(jax.random.fold_in(own_key, 6), position), (parts,), jnp.float32, smallest / len(cuts), largest / len(cuts))
        loudness = loudness * jnp.repeat(jnp.exp(steps), dims[position] // parts).reshape((-1,) + (1,) * (len(dims) - 1 - position))
    return loudness


def gaussian(rng, shape, deviation, bound, cuts=(), kind=jnp.bfloat16):
    values = deviation * jax.random.normal(rng, shape, jnp.float32)
    if cuts:
        values = values * block_levels(rng, shape, cuts, -0.22, 0.18)
    return jnp.clip(values, -bound, bound).astype(kind)


def setup_inputs(seed: int = 0) -> dict:
    key_of = jax.random.split(jax.random.key(seed), 12)
    features = gaussian(key_of[0], (NATOM, F), 1.0, 6.0, ((0, 512),))
    positions = draw_positions(jax.random.fold_in(key_of[11], 71), 0)
    cluster_atoms = draw_cluster_atoms(jax.random.fold_in(key_of[11], 71), 0)
    pair_cells = draw_pair_cells(jax.random.fold_in(key_of[11], 71), 0)
    pair_count = draw_pair_count(jax.random.fold_in(key_of[11], 71), 0)
    project_weight = gaussian(key_of[5], (F, F), F ** -0.5, 0.25)
    basis_filter = gaussian(key_of[6], (NRBF, F), (2 * CL) ** -0.5, 0.375, (), jnp.float32)
    hidden_weight = gaussian(key_of[7], (F, F), F ** -0.5, 0.25)
    hidden_bias = gaussian(key_of[8], (F,), 1.0, 4.0, (), jnp.float32)
    output_weight = gaussian(key_of[9], (F, F), F ** -0.5, 0.25)
    output_bias = gaussian(key_of[10], (F,), 0.5, 3.0, (), jnp.float32)
    return dict(features=features, positions=positions, cluster_atoms=cluster_atoms, pair_cells=pair_cells, pair_count=pair_count, project_weight=project_weight, basis_filter=basis_filter, hidden_weight=hidden_weight, hidden_bias=hidden_bias, output_weight=output_weight, output_bias=output_bias)


cutoff_radius = 5.0

def basis_weights(target_pos, source_pos, target_first, source_first, source_valid, basis_count):
    cluster = target_pos.shape[1]
    squared = jnp.zeros((cluster, cluster), jnp.float32)
    for component in range(3):
        difference = target_pos[component][:, None] - source_pos[component][None, :]
        squared = squared + difference * difference
    distance = jnp.sqrt(squared)
    target_ids = target_first + lax.broadcasted_iota(jnp.int32, (cluster, cluster), 0)
    source_local = lax.broadcasted_iota(jnp.int32, (cluster, cluster), 1)
    allowed = (target_ids != source_first + source_local) & (source_local < source_valid) & (distance < cutoff_radius)
    smooth = 0.5 * (jnp.cos(math.pi / cutoff_radius * distance) + 1.0)
    envelope = jnp.where(allowed, smooth, 0.0)
    centers = lax.broadcasted_iota(jnp.int32, (1, basis_count, 1), 1).astype(jnp.float32) * (cutoff_radius / (basis_count - 1))
    sharpness = ((basis_count - 1) / cutoff_radius) ** 2
    offset = distance[:, None, :] - centers
    weights = jnp.exp(-sharpness * offset * offset) * envelope[:, None, :]
    return weights.astype(jnp.bfloat16).reshape(cluster, basis_count * cluster)

def scaled_sources(source_rows, basis_filter):
    scaled = basis_filter[:, None, :] * source_rows[None, :, :].astype(jnp.float32)
    return scaled.astype(jnp.bfloat16).reshape(-1, source_rows.shape[1])

def refine(message, first_atom, cluster_atoms, hidden_weight, hidden_bias, output_weight, output_bias, cluster):
    rounded = message.astype(jnp.bfloat16)
    hidden = jnp.dot(rounded, hidden_weight, preferred_element_type=jnp.float32) + hidden_bias
    hidden = (jax.nn.softplus(hidden) - math.log(2.0)).astype(jnp.bfloat16)
    result = jnp.dot(hidden, output_weight, preferred_element_type=jnp.float32) + output_bias
    row_total = message.shape[0]
    atom_ids = first_atom + lax.broadcasted_iota(jnp.int32, (row_total, 1), 0)
    cluster_ids = atom_ids // cluster
    table_ids = lax.broadcasted_iota(jnp.int32, (1, cluster_atoms.shape[0]), 1)
    valid_atoms = lax.optimization_barrier(jnp.sum(jnp.where(cluster_ids == table_ids, cluster_atoms[None, :], 0), axis=1, keepdims=True))
    keeping = atom_ids - cluster_ids * cluster < valid_atoms
    return jnp.where(keeping, result, 0.0).astype(jnp.bfloat16)

def reference(features, positions, cluster_atoms, pair_cells, pair_count, project_weight, basis_filter, hidden_weight, hidden_bias, output_weight, output_bias):
    projected = jnp.dot(features, project_weight, preferred_element_type=jnp.float32).astype(jnp.bfloat16)
    messages = jnp.zeros((positions.shape[1], F), jnp.float32)

    def device_step(device, running_all):
        device_id = jnp.asarray(device).astype(jnp.int32)
        row_index = device_id // N_COL
        col_index = device_id - row_index * N_COL
        listed = pair_count[row_index, col_index]

        def add_pair(slot_index, running):
            pair_cell = pair_cells[row_index, col_index, slot_index]
            target_local = pair_cell // SPC
            source_local = pair_cell - target_local * SPC
            target_first = ((row_index * CPR + target_local) * CL).astype(jnp.int32)
            source_cluster = (col_index * SPC + source_local).astype(jnp.int32)
            source_first = (source_cluster * CL).astype(jnp.int32)
            target_pos = lax.dynamic_slice_in_dim(positions, target_first, CL, 1)
            source_pos = lax.dynamic_slice_in_dim(positions, source_first, CL, 1)
            source_valid = cluster_atoms[source_cluster]
            weights = basis_weights(target_pos, source_pos, target_first, source_first, source_valid, NRBF)
            source_rows = lax.dynamic_slice_in_dim(projected, source_first, CL, 0)
            message = jnp.dot(weights, scaled_sources(source_rows, basis_filter), preferred_element_type=jnp.float32)
            current = lax.dynamic_slice_in_dim(running, target_first, CL, 0)
            return lax.dynamic_update_slice_in_dim(running, current + message, target_first, 0)
        return lax.fori_loop(0, listed, add_pair, running_all)
    messages = lax.fori_loop(0, N_ROW * N_COL, device_step, messages)
    return refine(messages, 0, cluster_atoms, hidden_weight, hidden_bias, output_weight, output_bias, CL)
```

```python
import functools
import math

import jax
import jax.numpy as jnp
from jax import lax
from jax.experimental import pallas as pl
from jax.experimental.pallas import tpu as pltpu
from jax.sharding import PartitionSpec as P

CL = 128
F = 512
NRBF = 16
CUTOFF = 5.0
MESH = pl.DeviceIdType.MESH
VMEM_LIMIT = 56 * 1024 * 1024


def vmem():
    return pl.BlockSpec(memory_space=pltpu.VMEM)


def smem():
    return pl.BlockSpec(memory_space=pltpu.SMEM)


def hbm():
    return pl.BlockSpec(memory_space=pl.ANY)


def gather_kernel(n_row, x_ref, w_ref, out_ref, send_sem, recv_sem, fwd_sem):
    me = lax.axis_index("row")
    core = lax.rem(me, 2)
    chip = lax.div(me, 2)
    chips = n_row // 2
    sibling = me + 1 - 2 * core

    def peer(j):
        return lax.rem(chip + j, chips) * 2 + core

    barrier = pltpu.get_barrier_semaphore()
    for j in range(1, chips):
        pl.semaphore_signal(barrier, inc=1, device_id={"row": peer(j)}, device_id_type=MESH)
    pl.semaphore_signal(barrier, inc=1, device_id={"row": sibling}, device_id_type=MESH)
    out_ref[me] = jnp.dot(x_ref[...], w_ref[...], preferred_element_type=jnp.float32).astype(
        jnp.bfloat16
    )
    pl.semaphore_wait(barrier, chips)

    def direct(j):
        return pltpu.make_async_remote_copy(
            src_ref=out_ref.at[me],
            dst_ref=out_ref.at[me],
            send_sem=send_sem.at[j],
            recv_sem=recv_sem.at[me],
            device_id={"row": peer(j)},
            device_id_type=MESH,
        )

    def forward(block, j):
        return pltpu.make_async_remote_copy(
            src_ref=out_ref.at[block],
            dst_ref=out_ref.at[block],
            send_sem=fwd_sem.at[j],
            recv_sem=recv_sem.at[block],
            device_id={"row": sibling},
            device_id_type=MESH,
        )

    def arrived(block):
        pltpu.make_async_remote_copy(
            src_ref=out_ref.at[block],
            dst_ref=out_ref.at[block],
            send_sem=send_sem.at[0],
            recv_sem=recv_sem.at[block],
            device_id={"row": sibling},
            device_id_type=MESH,
        ).wait_recv()

    for j in range(1, chips):
        direct(j).start()
    forward(me, 0).start()
    for j in range(1, chips):
        block = lax.rem(chip + chips - j, chips) * 2 + core
        arrived(block)
        forward(block, j).start()
    for j in range(chips):
        arrived(lax.rem(chip + chips - j, chips) * 2 + 1 - core)
    for j in range(1, chips):
        direct(j).wait_send()
    for j in range(chips):
        forward(lax.rem(chip + chips - j, chips) * 2 + core, j).wait_send()


def gather_projected(features, weight, n_row):
    rows = features.shape[0]
    return pl.pallas_call(
        functools.partial(gather_kernel, n_row),
        out_shape=jax.ShapeDtypeStruct((n_row, rows, F), jnp.bfloat16),
        in_specs=[vmem(), vmem()],
        out_specs=vmem(),
        scratch_shapes=[
            pltpu.SemaphoreType.DMA((n_row // 2,)),
            pltpu.SemaphoreType.DMA((n_row,)),
            pltpu.SemaphoreType.DMA((n_row // 2,)),
        ],
        compiler_params=pltpu.CompilerParams(
            collective_id=0, has_side_effects=True, vmem_limit_bytes=VMEM_LIMIT
        ),
        name="project_gather",
    )(features, weight)


def envelope_of(squared):
    x = squared * (math.pi / (2.0 * CUTOFF)) ** 2
    coefficients = [(-1.0) ** n / math.factorial(2 * n) for n in range(8)]
    value = jnp.full_like(x, coefficients[-1])
    for c in coefficients[-2::-1]:
        value = value * x + c
    return value * value


def pair_kernel(
    clusters,
    per_row,
    cells_ref,
    count_ref,
    atoms_ref,
    pos_ref,
    filter_ref,
    source_ref,
    out_ref,
    tpos,
    spos,
    weights,
    scaled,
    sem,
):
    row = lax.axis_index("row")
    col = lax.axis_index("col")
    first = pltpu.make_async_copy(
        pos_ref.at[:, pl.ds(pl.multiple_of(row * per_row * CL, CL), per_row * CL)],
        tpos.at[pl.ds(0, 3)],
        sem.at[0],
    )
    second = pltpu.make_async_copy(
        pos_ref.at[:, pl.ds(pl.multiple_of(col * clusters * CL, CL), clusters * CL)],
        spos.at[pl.ds(0, 3)],
        sem.at[1],
    )
    tpos[...] = jnp.zeros_like(tpos)
    first.start()
    second.start()
    out_ref[...] = jnp.zeros_like(out_ref)
    first.wait()
    second.wait()
    spread = math.sqrt(math.log2(math.e))

    def job(slot, carry):
        cell = cells_ref[0, 0, slot]
        target = lax.div(cell, clusters)
        source = cell - target * clusters
        target_at = pl.multiple_of(target * CL, CL)
        source_at = pl.multiple_of(source * CL, CL)
        across = jnp.transpose(tpos[:, pl.ds(target_at, CL)])
        along = spos[:, pl.ds(source_at, CL)]
        squared = jnp.zeros((CL, CL), jnp.float32)
        for component in range(3):
            difference = across[:, component : component + 1] - along[component : component + 1, :]
            squared = squared + difference * difference
        distance = jnp.sqrt(squared)
        target_ids = (row * per_row + target) * CL + lax.broadcasted_iota(jnp.int32, (CL, CL), 0)
        local = lax.broadcasted_iota(jnp.int32, (CL, CL), 1)
        source_cluster = col * clusters + source
        allowed = (
            (target_ids != source_cluster * CL + local)
            & (local < atoms_ref[source_cluster])
            & (distance < CUTOFF)
        )
        envelope = jnp.where(allowed, envelope_of(squared), 0.0)
        reach = distance * ((NRBF - 1) / CUTOFF * spread)
        rows = source_ref[pl.ds(source_at, CL), :].astype(jnp.float32)
        for k in range(NRBF):
            offset = reach - k * spread
            weights[:, k * CL : (k + 1) * CL] = (jnp.exp2(-(offset * offset)) * envelope).astype(
                jnp.bfloat16
            )
            scaled[k * CL : (k + 1) * CL, :] = (filter_ref[k : k + 1, :] * rows).astype(jnp.bfloat16)
        out_ref[pl.ds(target_at, CL), :] += jnp.dot(
            weights[...], scaled[...], preferred_element_type=jnp.float32
        )
        return carry

    lax.fori_loop(0, count_ref[0, 0], job, 0)


def pair_messages(cells, count, atoms, positions, basis_filter, source, per_row):
    clusters = source.shape[0] // CL
    return pl.pallas_call(
        functools.partial(pair_kernel, clusters, per_row),
        out_shape=jax.ShapeDtypeStruct((per_row * CL, F), jnp.float32),
        in_specs=[smem(), smem(), smem(), hbm(), vmem(), vmem()],
        out_specs=vmem(),
        scratch_shapes=[
            pltpu.VMEM((8, per_row * CL), jnp.float32),
            pltpu.VMEM((8, clusters * CL), jnp.float32),
            pltpu.VMEM((CL, NRBF * CL), jnp.bfloat16),
            pltpu.VMEM((NRBF * CL, F), jnp.bfloat16),
            pltpu.SemaphoreType.DMA((2,)),
        ],
        compiler_params=pltpu.CompilerParams(vmem_limit_bytes=VMEM_LIMIT),
        name="pair_messages",
    )(cells, count, atoms, positions, basis_filter, source)


CH = 4
CW = F // CH


def finish_kernel(
    nz,
    m_ref,
    atoms_ref,
    hw_ref,
    hb_ref,
    ow_ref,
    ob_ref,
    out_ref,
    rs,
    stage,
    xsend,
    xrecv,
    out_v,
    rs_send,
    rs_recv,
    x_sem,
    ag_send,
    ag_recv,
    out_sem,
):
    row = lax.axis_index("row")
    col = lax.axis_index("col")
    h = lax.div(col, nz)
    z = lax.rem(col, nz)
    far = nz // 2
    neighbour = (h * nz + lax.rem(z + 1, nz), h * nz + lax.rem(z + nz - 1, nz))
    partner = (1 - h) * nz + z

    barrier = pltpu.get_barrier_semaphore()
    for other in neighbour + (partner,):
        pl.semaphore_signal(barrier, inc=1, device_id={"col": other}, device_id_type=MESH)
    pl.semaphore_wait(barrier, 3)

    def ahead(way, d):
        return lax.rem(z + d, nz) if way == 0 else lax.rem(z + nz - d, nz)

    def mine(t, c):
        return m_ref[pl.ds(pl.multiple_of(t * CL, CL), CL), c * CW : (c + 1) * CW]

    def long(way, c):
        return (c < CH // 2) == (way == 0)

    def rs_copy(way, c, k, src):
        return pltpu.make_async_remote_copy(
            src_ref=src,
            dst_ref=rs.at[way, k, c],
            send_sem=rs_send.at[way, c, k],
            recv_sem=rs_recv.at[way, c, k],
            device_id={"col": neighbour[way]},
            device_id_type=MESH,
        )

    order = [(way, c if way == 0 else CH - 1 - c) for c in range(CH) for way in range(2)]

    def begin(way, c, k):
        stage[way, c] = mine(ahead(way, far - k), c).astype(jnp.bfloat16)
        rs_copy(way, c, k, stage.at[way, c]).start()

    def relay(way, c, k):
        rs_copy(way, c, k - 1, rs.at[way, k - 1, c]).wait_recv()
        total = rs[way, k - 1, c].astype(jnp.float32) + mine(ahead(way, far - k), c)
        rs[way, k - 1, c] = total.astype(jnp.bfloat16)
        rs_copy(way, c, k, rs.at[way, k - 1, c]).start()

    for way, c in order:
        if long(way, c):
            begin(way, c, 0)
    for way, c in order:
        if not long(way, c):
            begin(way, c, 1)
    for way, c in order:
        if long(way, c):
            relay(way, c, 1)

    def step(k, carry):
        for way, c in order:
            relay(way, c, k)
        return carry

    lax.fori_loop(2, far, step, 0)

    half = CL // 2
    for c in range(CH):
        for way in range(2):
            rs_copy(way, c, far - 1, rs.at[way, far - 1, c]).wait_recv()
        total = (
            rs[0, far - 1, c].astype(jnp.float32)
            + rs[1, far - 1, c].astype(jnp.float32)
            + mine(z, c)
        )
        xsend[0, :, c * CW : (c + 1) * CW] = total[:half].astype(jnp.bfloat16)
        xsend[1, :, c * CW : (c + 1) * CW] = total[half:].astype(jnp.bfloat16)
    cross = pltpu.make_async_remote_copy(
        src_ref=xsend.at[1 - h],
        dst_ref=xrecv,
        send_sem=x_sem.at[0],
        recv_sem=x_sem.at[1],
        device_id={"col": partner},
        device_id_type=MESH,
    )
    cross.start()

    for way, c in order:
        if long(way, c):
            rs_copy(way, c, 0, stage.at[way, c]).wait_send()

    def sent(k, carry):
        for way, c in order:
            rs_copy(way, c, k, stage.at[way, c]).wait_send()
        return carry

    lax.fori_loop(1, far, sent, 0)
    cross.wait_recv()

    message = (xsend[h].astype(jnp.float32) + xrecv[...].astype(jnp.float32)).astype(jnp.bfloat16)
    hidden = jnp.dot(message, hw_ref[...], preferred_element_type=jnp.float32) + hb_ref[...]
    hidden = jnp.maximum(hidden, 0.0) + jnp.log1p(jnp.exp(-jnp.abs(hidden))) - math.log(2.0)
    result = (
        jnp.dot(hidden.astype(jnp.bfloat16), ow_ref[...], preferred_element_type=jnp.float32)
        + ob_ref[...]
    )
    atom = h * half + lax.broadcasted_iota(jnp.int32, (half, F), 0)
    valid = atoms_ref[row * nz + z]
    out_v[z, h] = jnp.where(atom < valid, result, 0.0).astype(jnp.bfloat16)
    cross.wait_send()

    swap = pltpu.make_async_remote_copy(
        src_ref=out_v.at[z, h],
        dst_ref=out_v.at[z, h],
        send_sem=x_sem.at[2],
        recv_sem=x_sem.at[3],
        device_id={"col": partner},
        device_id_type=MESH,
    )
    swap.start()

    def block(t, j):
        return out_v.at[t, h if j == 0 else 1 - h]

    def ag_copy(way, j, k):
        ref = block(ahead(1 - way, k), j)
        return pltpu.make_async_remote_copy(
            src_ref=ref,
            dst_ref=ref,
            send_sem=ag_send.at[way, j, k],
            recv_sem=ag_recv.at[way, j, k],
            device_id={"col": neighbour[way]},
            device_id_type=MESH,
        )

    def ag_arrived(way, j, k):
        ref = block(ahead(1 - way, k + 1), j)
        pltpu.make_async_remote_copy(
            src_ref=ref,
            dst_ref=ref,
            send_sem=ag_send.at[way, j, k],
            recv_sem=ag_recv.at[way, j, k],
            device_id={"col": neighbour[way]},
            device_id_type=MESH,
        ).wait_recv()

    def store(t, j):
        half_index = h if j == 0 else 1 - h
        return pltpu.make_async_copy(
            out_v.at[t, half_index], out_ref.at[t, half_index], out_sem.at[t, half_index]
        )

    def ag_long(way, j):
        return way == j

    for way in range(2):
        ag_copy(way, 0, 0).start()
    store(z, 0).start()
    swap_in = pltpu.make_async_remote_copy(
        src_ref=block(z, 1),
        dst_ref=block(z, 1),
        send_sem=x_sem.at[2],
        recv_sem=x_sem.at[3],
        device_id={"col": partner},
        device_id_type=MESH,
    )
    swap_in.wait_recv()
    for way in range(2):
        ag_copy(way, 1, 0).start()
    store(z, 1).start()

    def ag_step(k, carry):
        for j in range(2):
            for way in range(2):
                ag_arrived(way, j, k - 1)
                ag_copy(way, j, k).start()
                store(ahead(1 - way, k), j).start()
        return carry

    lax.fori_loop(1, far - 1, ag_step, 0)
    for j in range(2):
        for way in range(2):
            ag_arrived(way, j, far - 2)
            if ag_long(way, j):
                ag_copy(way, j, far - 1).start()
            store(ahead(1 - way, far - 1), j).start()
    for j in range(2):
        way = j
        ag_arrived(way, j, far - 1)
        store(ahead(1 - way, far), j).start()

    swap.wait_send()

    def ag_sent(k, carry):
        for j in range(2):
            for way in range(2):
                ag_copy(way, j, k).wait_send()
        return carry

    lax.fori_loop(0, far - 1, ag_sent, 0)
    for j in range(2):
        ag_copy(j, j, far - 1).wait_send()

    def stored(t, carry):
        for j in range(2):
            store(t, j).wait()
        return carry

    lax.fori_loop(0, nz, stored, 0)


def finish(message, atoms, hidden_weight, hidden_bias, output_weight, output_bias, n_col):
    nz = message.shape[0] // CL
    far = nz // 2
    return pl.pallas_call(
        functools.partial(finish_kernel, nz),
        out_shape=jax.ShapeDtypeStruct((nz, 2, CL // 2, F), jnp.bfloat16),
        in_specs=[vmem(), smem(), vmem(), vmem(), vmem(), vmem()],
        out_specs=hbm(),
        scratch_shapes=[
            pltpu.VMEM((2, far, CH, CL, CW), jnp.bfloat16),
            pltpu.VMEM((2, CH, CL, CW), jnp.bfloat16),
            pltpu.VMEM((2, CL // 2, F), jnp.bfloat16),
            pltpu.VMEM((CL // 2, F), jnp.bfloat16),
            pltpu.VMEM((nz, 2, CL // 2, F), jnp.bfloat16),
            pltpu.SemaphoreType.DMA((2, CH, far)),
            pltpu.SemaphoreType.DMA((2, CH, far)),
            pltpu.SemaphoreType.DMA((4,)),
            pltpu.SemaphoreType.DMA((2, 2, far)),
            pltpu.SemaphoreType.DMA((2, 2, far)),
            pltpu.SemaphoreType.DMA((nz, 2)),
        ],
        compiler_params=pltpu.CompilerParams(
            collective_id=1, has_side_effects=True, vmem_limit_bytes=VMEM_LIMIT
        ),
        name="sum_update_gather",
    )(message, atoms, hidden_weight, hidden_bias, output_weight, output_bias)


def local(
    n_row,
    n_col,
    features,
    positions,
    cluster_atoms,
    pair_cells,
    pair_count,
    project_weight,
    basis_filter,
    hidden_weight,
    hidden_bias,
    output_weight,
    output_bias,
):
    per_row = positions.shape[1] // CL // n_row
    projected = gather_projected(features, project_weight, n_row).reshape(-1, F)
    message = pair_messages(
        pair_cells, pair_count, cluster_atoms, positions, basis_filter, projected, per_row
    )
    update = finish(
        message,
        cluster_atoms,
        hidden_weight,
        hidden_bias.reshape(1, F),
        output_weight,
        output_bias.reshape(1, F),
        n_col,
    )
    return update.reshape(-1, F)


def solution(mesh):
    in_specs = (
        P(("col", "row"), None),
        P(),
        P(),
        P("row", "col", None),
        P("row", "col"),
        P(),
        P(),
        P(),
        P(),
        P(),
        P(),
    )
    out_specs = P("row", None)
    body = functools.partial(local, mesh.shape["row"], mesh.shape["col"])
    return jax.shard_map(body, mesh=mesh, in_specs=in_specs, out_specs=out_specs, check_vma=False)
```

```python
import functools
import math

import jax
import jax.numpy as jnp
from jax import lax
from jax.experimental import pallas as pl
from jax.experimental.pallas import tpu as pltpu
from jax.sharding import PartitionSpec as P

CL = 128
F = 512
NRBF = 16
CUTOFF = 5.0
MESH = pl.DeviceIdType.MESH
VMEM_LIMIT = 56 * 1024 * 1024


HALF = CL // 2
HF = F // 2


def vmem():
    return pl.BlockSpec(memory_space=pltpu.VMEM)


def smem():
    return pl.BlockSpec(memory_space=pltpu.SMEM)


def hbm():
    return pl.BlockSpec(memory_space=pl.ANY)


def envelope_of(squared):
    x = squared * (math.pi / (2.0 * CUTOFF)) ** 2
    coefficients = [(-1.0) ** n / math.factorial(2 * n) for n in range(8)]
    value = jnp.full_like(x, coefficients[-1])
    for c in coefficients[-2::-1]:
        value = value * x + c
    return value * value


def remote(src, dst, send, recv, device):
    return pltpu.make_async_remote_copy(
        src_ref=src,
        dst_ref=dst,
        send_sem=send,
        recv_sem=recv,
        device_id=device,
        device_id_type=MESH,
    )


def kernel(
    n_row,
    nz,
    clusters,
    slots,
    x_ref,
    pw_ref,
    cells_ref,
    count_ref,
    atoms_ref,
    pos_ref,
    filter_ref,
    hw_hbm,
    hb_ref,
    ow_hbm,
    ob_ref,
    out_ref,
    source,
    tpos,
    spos,
    tcols,
    srows,
    hw_ref,
    ow_ref,
    weights,
    scaled,
    jobs,
    xout,
    xin,
    tip_out,
    tip_in,
    far_in,
    near_in,
    zout,
    message,
    out_v,
    load_sem,
    row_send,
    row_recv,
    row_fwd,
    x_send,
    x_recv,
    tip_send,
    tip_recv,
    far_send,
    far_recv,
    near_send,
    near_recv,
    gx_send,
    gx_recv,
    gfar_send,
    gfar_recv,
    gnear_send,
    gnear_recv,
    out_sem,
):
    row = lax.axis_index("row")
    col = lax.axis_index("col")
    core = lax.rem(row, 2)
    chip = lax.div(row, 2)
    chips = n_row // 2
    h = lax.div(col, nz)
    z = lax.rem(col, nz)
    top = nz // 2
    ways = (0, 1)
    per_row = nz

    def in_row(index):
        return {"row": index}

    def in_col(index):
        return {"col": index}

    sibling = in_row(row + 1 - 2 * core)
    peers = [in_row(lax.rem(chip + j, chips) * 2 + core) for j in range(1, chips)]
    one = [
        in_col(h * nz + lax.rem(z + 1, nz)),
        in_col(h * nz + lax.rem(z + nz - 1, nz)),
    ]
    two = [
        in_col(h * nz + lax.rem(z + 2, nz)),
        in_col(h * nz + lax.rem(z + nz - 2, nz)),
    ]
    partner = in_col((1 - h) * nz + z)

    barrier = pltpu.get_barrier_semaphore()
    everyone = peers + [sibling] + one + two + [partner]
    for other in everyone:
        pl.semaphore_signal(barrier, inc=1, device_id=other, device_id_type=MESH)

    loads = [
        pltpu.make_async_copy(
            pos_ref.at[:, pl.ds(pl.multiple_of(row * per_row * CL, CL), per_row * CL)],
            tpos.at[pl.ds(0, 3)],
            load_sem.at[0],
        ),
        pltpu.make_async_copy(
            pos_ref.at[:, pl.ds(pl.multiple_of(col * clusters * CL, CL), clusters * CL)],
            spos.at[pl.ds(0, 3)],
            load_sem.at[1],
        ),
        pltpu.make_async_copy(hw_hbm, hw_ref, load_sem.at[2]),
        pltpu.make_async_copy(ow_hbm, ow_ref, load_sem.at[3]),
    ]
    tpos[...] = jnp.zeros_like(tpos)
    spos[...] = jnp.zeros_like(spos)
    for load in loads:
        load.start()

    source[chip, core] = jnp.dot(
        x_ref[...], pw_ref[...], preferred_element_type=jnp.float32
    ).astype(jnp.bfloat16)
    pl.semaphore_wait(barrier, len(everyone))

    def row_copy(c, k, send, device):
        ref = source.at[c, k]
        return remote(ref, ref, send, row_recv.at[c, k], device)

    def back(j):
        return lax.rem(chip + chips - j, chips)

    for j in range(1, chips):
        row_copy(chip, core, row_send.at[j], peers[j - 1]).start()
    row_copy(chip, core, row_fwd.at[0], sibling).start()

    targets = [lax.div(cells_ref[0, 0, slot], clusters) for slot in range(slots)]

    def last_of(t):
        found = slots
        for slot in range(slots):
            found = jnp.where(targets[slot] == t, slot, found)
        return found

    for q in range(2):
        jobs[q, slots] = jnp.zeros((CL, HF), jnp.float32)

    loads[0].wait()
    loads[1].wait()
    for t in range(per_row):
        tcols[t] = jnp.transpose(tpos[:, t * CL : (t + 1) * CL])
    for t in range(clusters):
        srows[t] = spos[:, t * CL : (t + 1) * CL]
    spread = math.sqrt(math.log2(math.e))

    def basis(slot, carry):
        cell = cells_ref[0, 0, slot]
        target = lax.div(cell, clusters)
        near_source = cell - target * clusters
        across = tcols[target]
        along = srows[near_source]
        squared = jnp.zeros((CL, CL), jnp.float32)
        for component in range(3):
            difference = across[:, component : component + 1] - along[component : component + 1, :]
            squared = squared + difference * difference
        distance = jnp.sqrt(squared)
        target_ids = (row * per_row + target) * CL + lax.broadcasted_iota(jnp.int32, (CL, CL), 0)
        local_ids = lax.broadcasted_iota(jnp.int32, (CL, CL), 1)
        source_cluster = col * clusters + near_source
        real = jnp.where(slot < count_ref[0, 0], atoms_ref[source_cluster], 0)
        allowed = (
            (target_ids != source_cluster * CL + local_ids)
            & (local_ids < real)
            & (distance < CUTOFF)
        )
        envelope = jnp.where(allowed, envelope_of(squared), 0.0)
        reach = distance * ((NRBF - 1) / CUTOFF * spread)
        for k in range(NRBF):
            offset = reach - k * spread
            weights[slot, :, k * CL : (k + 1) * CL] = (
                jnp.exp2(-(offset * offset)) * envelope
            ).astype(jnp.bfloat16)
        return carry

    early = slots * 2 // 3
    lax.fori_loop(0, early, basis, 0)
    for j in range(1, chips):
        row_copy(back(j), core, row_fwd.at[j], sibling).wait_recv()
        row_copy(back(j), core, row_fwd.at[j], sibling).start()
    lax.fori_loop(early, slots, basis, 0)
    for j in range(chips):
        row_copy(back(j), 1 - core, row_fwd.at[j], sibling).wait_recv()

    def ahead(way, d):
        return lax.rem(z + d, nz) if way == 0 else lax.rem(z + nz - d, nz)

    def behind(way, d):
        return ahead(1 - way, d)

    order = [(0, top)]
    for d in range(top - 1, 0, -2):
        pair = (d, d + 1) if d + 1 < top else (d,)
        order += [(way, e) for e in pair for way in ways]
    order += [(0, 0)]
    last = {(way, d): last_of(ahead(way, d)) for way, d in order}

    def mine(place, which, q):
        return jobs[q, last[place], pl.ds(pl.multiple_of(which * HALF, HALF), HALF), :]

    def x_copy(t, q):
        return remote(xout.at[t, q], xin.at[t, q], x_send.at[t, q], x_recv.at[t, q], partner)

    for q in range(2):
        columns = slice(q * HF, (q + 1) * HF)

        def scale(s, carry):
            rows = source[s, :, :, columns].reshape(CL, HF).astype(jnp.float32)
            for k in range(NRBF):
                scaled[s, k * CL : (k + 1) * CL, :] = (filter_ref[k : k + 1, columns] * rows).astype(
                    jnp.bfloat16
                )
            return carry

        lax.fori_loop(0, clusters, scale, 0)

        def job(slot, carry):
            cell = cells_ref[0, 0, slot]
            target = lax.div(cell, clusters)
            before = slots
            for other in range(slots - 1):
                before = jnp.where((targets[other] == target) & (other < slot), other, before)
            jobs[q, slot] = jobs[q, before] + jnp.dot(
                weights[slot],
                scaled[cell - target * clusters],
                preferred_element_type=jnp.float32,
            )
            return carry

        lax.fori_loop(0, slots, job, 0)
        for way, d in order:
            t = ahead(way, d)
            xout[t, q] = mine((way, d), 1 - h, q).astype(jnp.bfloat16)
            x_copy(t, q).start()

    def tip(q):
        return remote(tip_out.at[q], tip_in.at[q], tip_send.at[q], tip_recv.at[q], two[q])

    def near(way, d, q):
        i = (top - 1 - d) // 2
        return remote(
            zout.at[way, d - 1, q],
            near_in.at[way, i, q],
            near_send.at[way, i, q],
            near_recv.at[way, i, q],
            one[way],
        )

    def far(way, d, q):
        i = (top - 2 - d) // 2
        return remote(
            zout.at[way, d - 1, q],
            far_in.at[way, i, q],
            far_send.at[way, i, q],
            far_recv.at[way, i, q],
            two[way],
        )

    def come(way, d, q):
        near(way, d + 1, q).wait_recv()
        total = near_in[way, (top - 2 - d) // 2, q].astype(jnp.float32)
        if d + 2 == top:
            if way == q:
                tip(q).wait_recv()
                total = total + tip_in[q].astype(jnp.float32)
            return total
        far(way, d + 2, q).wait_recv()
        return total + far_in[way, (top - 4 - d) // 2, q].astype(jnp.float32)

    for q in range(2):
        for way, d in order:
            t = ahead(way, d)
            x_copy(t, q).wait_recv()
            total = mine((way, d), h, q) + xin[t, q].astype(jnp.float32)
            if d == top:
                tip_out[q] = total.astype(jnp.bfloat16)
                tip(q).start()
            elif d % 2:
                zout[way, d - 1, q] = total.astype(jnp.bfloat16)
                near(way, d, q).start()
            elif d:
                zout[way, d - 1, q] = (total + come(way, d, q)).astype(jnp.bfloat16)
                far(way, d, q).start()
            else:
                message[:, q * HF : (q + 1) * HF] = (total + come(0, 0, q) + come(1, 0, q)).astype(
                    jnp.bfloat16
                )

    loads[2].wait()
    loads[3].wait()
    hidden = jnp.dot(message[...], hw_ref[...], preferred_element_type=jnp.float32) + hb_ref[...]
    hidden = jnp.maximum(hidden, 0.0) + jnp.log1p(jnp.exp(-jnp.abs(hidden))) - math.log(2.0)
    result = (
        jnp.dot(hidden.astype(jnp.bfloat16), ow_ref[...], preferred_element_type=jnp.float32)
        + ob_ref[...]
    )
    atom = h * HALF + lax.broadcasted_iota(jnp.int32, (HALF, F), 0)
    valid = atoms_ref[row * per_row + z]
    out_v[z, h] = jnp.where(atom < valid, result, 0.0).astype(jnp.bfloat16)

    def g_near(way, e):
        ref = out_v.at[behind(way, e), h]
        i = e // 2
        return remote(ref, ref, gnear_send.at[way, i], gnear_recv.at[way, i], one[way])

    def g_far(way, e):
        i = e // 2
        if e + 2 == top:
            ref = out_v.at[behind(way, e), h, pl.ds(way * (HALF // 2), HALF // 2)]
        else:
            ref = out_v.at[behind(way, e), h]
        return remote(ref, ref, gfar_send.at[way, i], gfar_recv.at[way, i], two[way])

    def g_near_in(way, e):
        ref = out_v.at[behind(way, e + 1), h]
        i = e // 2
        remote(ref, ref, gnear_send.at[way, i], gnear_recv.at[way, i], one[way]).wait_recv()

    def g_far_in(way, e):
        i = e // 2
        if e + 2 == top:
            ref = out_v.at[behind(way, e + 2), h, pl.ds(way * (HALF // 2), HALF // 2)]
        else:
            ref = out_v.at[behind(way, e + 2), h]
        remote(ref, ref, gfar_send.at[way, i], gfar_recv.at[way, i], two[way]).wait_recv()

    def cross(t, which):
        ref = out_v.at[t, which]
        return remote(ref, ref, gx_send.at[t], gx_recv.at[t], partner)

    def store(t, which):
        return pltpu.make_async_copy(out_v.at[t, which], out_ref.at[t, which], out_sem.at[t, which])

    def keep(t):
        cross(t, h).start()
        store(t, h).start()

    for way in ways:
        g_far(way, 0).start()
    for way in ways:
        g_near(way, 0).start()
    keep(z)
    for e in range(2, top + 1, 2):
        for way in ways:
            g_far_in(way, e - 2)
            if e < top:
                g_far(way, e).start()
                g_near(way, e).start()
                keep(behind(way, e))
        if e == top:
            keep(behind(0, top))
        for way in ways:
            g_near_in(way, e - 2)
            keep(behind(way, e - 1))

    arrive = [z]
    for e in range(2, top, 2):
        arrive += [behind(way, e) for way in ways] + [behind(way, e - 1) for way in ways]
    arrive += [behind(0, top)] + [behind(way, top - 1) for way in ways]
    for t in arrive:
        cross(t, 1 - h).wait_recv()
        store(t, 1 - h).start()

    for j in range(1, chips):
        row_copy(chip, core, row_send.at[j], peers[j - 1]).wait_send()
    for j in range(chips):
        row_copy(back(j), core, row_fwd.at[j], sibling).wait_send()
    for w in ways:
        tip(w).wait_send()
        for q in range(2):
            for d in range(1, top):
                (near if d % 2 else far)(w, d, q).wait_send()
        for e in range(0, top, 2):
            g_near(w, e).wait_send()
            g_far(w, e).wait_send()

    def ended(t, carry):
        for which in range(2):
            x_copy(t, which).wait_send()
            store(t, which).wait()
        cross(t, h).wait_send()
        return carry

    lax.fori_loop(0, nz, ended, 0)


def local(
    n_row,
    n_col,
    features,
    positions,
    cluster_atoms,
    pair_cells,
    pair_count,
    project_weight,
    basis_filter,
    hidden_weight,
    hidden_bias,
    output_weight,
    output_bias,
):
    rows = features.shape[0]
    slots = pair_cells.shape[2]
    clusters = n_row * rows // CL
    nz = positions.shape[1] // CL // n_row
    top = nz // 2
    steps = top // 2
    bf16 = jnp.bfloat16
    dma = pltpu.SemaphoreType.DMA
    update = pl.pallas_call(
        functools.partial(kernel, n_row, nz, clusters, slots),
        out_shape=jax.ShapeDtypeStruct((nz, 2, HALF, F), bf16),
        in_specs=[
            vmem(),
            vmem(),
            smem(),
            smem(),
            smem(),
            hbm(),
            vmem(),
            hbm(),
            vmem(),
            hbm(),
            vmem(),
        ],
        out_specs=hbm(),
        scratch_shapes=[
            pltpu.VMEM((n_row // 2, 2, rows, F), bf16),
            pltpu.VMEM((8, nz * CL), jnp.float32),
            pltpu.VMEM((8, clusters * CL), jnp.float32),
            pltpu.VMEM((nz, CL, 8), jnp.float32),
            pltpu.VMEM((clusters, 8, CL), jnp.float32),
            pltpu.VMEM((F, F), bf16),
            pltpu.VMEM((F, F), bf16),
            pltpu.VMEM((slots, CL, NRBF * CL), bf16),
            pltpu.VMEM((clusters, NRBF * CL, HF), bf16),
            pltpu.VMEM((2, slots + 1, CL, HF), jnp.float32),
            pltpu.VMEM((nz, 2, HALF, HF), bf16),
            pltpu.VMEM((nz, 2, HALF, HF), bf16),
            pltpu.VMEM((2, HALF, HF), bf16),
            pltpu.VMEM((2, HALF, HF), bf16),
            pltpu.VMEM((2, steps - 1, 2, HALF, HF), bf16),
            pltpu.VMEM((2, steps, 2, HALF, HF), bf16),
            pltpu.VMEM((2, top - 1, 2, HALF, HF), bf16),
            pltpu.VMEM((HALF, F), bf16),
            pltpu.VMEM((nz, 2, HALF, F), bf16),
            dma((4,)),
            dma((n_row // 2,)),
            dma((n_row // 2, 2)),
            dma((n_row // 2,)),
            dma((nz, 2)),
            dma((nz, 2)),
            dma((2,)),
            dma((2,)),
            dma((2, steps - 1, 2)),
            dma((2, steps - 1, 2)),
            dma((2, steps, 2)),
            dma((2, steps, 2)),
            dma((nz,)),
            dma((nz,)),
            dma((2, steps)),
            dma((2, steps)),
            dma((2, steps)),
            dma((2, steps)),
            dma((nz, 2)),
        ],
        compiler_params=pltpu.CompilerParams(
            collective_id=0, has_side_effects=True, vmem_limit_bytes=VMEM_LIMIT
        ),
        name="interaction",
    )(
        features,
        project_weight,
        pair_cells,
        pair_count,
        cluster_atoms,
        positions,
        basis_filter,
        hidden_weight,
        hidden_bias.reshape(1, F),
        output_weight,
        output_bias.reshape(1, F),
    )
    return update.reshape(-1, F)


def solution(mesh):
    in_specs = (
        P(("col", "row"), None),
        P(),
        P(),
        P("row", "col", None),
        P("row", "col"),
        P(),
        P(),
        P(),
        P(),
        P(),
        P(),
    )
    out_specs = P("row", None)
    body = functools.partial(local, mesh.shape["row"], mesh.shape["col"])
    return jax.shard_map(body, mesh=mesh, in_specs=in_specs, out_specs=out_specs, check_vma=False)
```

```python
import functools
import math

import jax
import jax.numpy as jnp
from jax import lax
from jax.experimental import pallas as pl
from jax.experimental.pallas import tpu as pltpu
from jax.sharding import PartitionSpec as P

CL = 128
F = 512
NRBF = 16
CUTOFF = 5.0
MESH = pl.DeviceIdType.MESH
VMEM_LIMIT = 56 * 1024 * 1024


HALF = CL // 2
HF = F // 2


def vmem():
    return pl.BlockSpec(memory_space=pltpu.VMEM)


def smem():
    return pl.BlockSpec(memory_space=pltpu.SMEM)


def hbm():
    return pl.BlockSpec(memory_space=pl.ANY)


def envelope_of(squared):
    x = squared * (math.pi / (2.0 * CUTOFF)) ** 2
    coefficients = [(-1.0) ** n / math.factorial(2 * n) for n in range(8)]
    value = jnp.full_like(x, coefficients[-1])
    for c in coefficients[-2::-1]:
        value = value * x + c
    return value * value


def remote(src, dst, send, recv, device):
    return pltpu.make_async_remote_copy(
        src_ref=src,
        dst_ref=dst,
        send_sem=send,
        recv_sem=recv,
        device_id=device,
        device_id_type=MESH,
    )


def kernel(
    n_row,
    nz,
    clusters,
    slots,
    x_ref,
    pw_ref,
    cells_ref,
    count_ref,
    atoms_ref,
    pos_ref,
    filter_ref,
    hw_hbm,
    hb_ref,
    ow_hbm,
    ob_ref,
    out_ref,
    source,
    tpos,
    spos,
    tcols,
    srows,
    hw_ref,
    ow_ref,
    weights,
    scaled,
    jobs,
    xout,
    xin,
    tip_out,
    tip_in,
    far_in,
    near_in,
    zout,
    message,
    out_v,
    load_sem,
    row_send,
    row_recv,
    row_fwd,
    x_send,
    x_recv,
    tip_send,
    tip_recv,
    far_send,
    far_recv,
    near_send,
    near_recv,
    gx_send,
    gx_recv,
    gfar_send,
    gfar_recv,
    gnear_send,
    gnear_recv,
    out_sem,
):
    row = lax.axis_index("row")
    col = lax.axis_index("col")
    core = lax.rem(row, 2)
    chip = lax.div(row, 2)
    chips = n_row // 2
    h = lax.div(col, nz)
    z = lax.rem(col, nz)
    top = nz // 2
    ways = (0, 1)
    per_row = nz

    def in_row(index):
        return {"row": index}

    def in_col(index):
        return {"col": index}

    sibling = in_row(row + 1 - 2 * core)
    peers = [in_row(lax.rem(chip + j, chips) * 2 + core) for j in range(1, chips)]
    one = [
        in_col(h * nz + lax.rem(z + 1, nz)),
        in_col(h * nz + lax.rem(z + nz - 1, nz)),
    ]
    two = [
        in_col(h * nz + lax.rem(z + 2, nz)),
        in_col(h * nz + lax.rem(z + nz - 2, nz)),
    ]
    partner = in_col((1 - h) * nz + z)

    barrier = pltpu.get_barrier_semaphore()
    everyone = peers + [sibling] + one + two + [partner]
    for other in everyone:
        pl.semaphore_signal(barrier, inc=1, device_id=other, device_id_type=MESH)

    loads = [
        pltpu.make_async_copy(
            pos_ref.at[:, pl.ds(pl.multiple_of(row * per_row * CL, CL), per_row * CL)],
            tpos.at[pl.ds(0, 3)],
            load_sem.at[0],
        ),
        pltpu.make_async_copy(
            pos_ref.at[:, pl.ds(pl.multiple_of(col * clusters * CL, CL), clusters * CL)],
            spos.at[pl.ds(0, 3)],
            load_sem.at[1],
        ),
        pltpu.make_async_copy(hw_hbm, hw_ref, load_sem.at[2]),
        pltpu.make_async_copy(ow_hbm, ow_ref, load_sem.at[3]),
    ]
    tpos[...] = jnp.zeros_like(tpos)
    spos[...] = jnp.zeros_like(spos)
    for load in loads:
        load.start()

    source[chip, core] = jnp.dot(
        x_ref[...], pw_ref[...], preferred_element_type=jnp.float32
    ).astype(jnp.bfloat16)
    pl.semaphore_wait(barrier, len(everyone))

    def row_copy(c, k, send, device):
        ref = source.at[c, k]
        return remote(ref, ref, send, row_recv.at[c, k], device)

    def back(j):
        return lax.rem(chip + chips - j, chips)

    for j in range(1, chips):
        row_copy(chip, core, row_send.at[j], peers[j - 1]).start()
    row_copy(chip, core, row_fwd.at[0], sibling).start()

    targets = [lax.div(cells_ref[0, 0, slot], clusters) for slot in range(slots)]

    def last_of(t):
        found = slots
        for slot in range(slots):
            found = jnp.where(targets[slot] == t, slot, found)
        return found

    for q in range(2):
        jobs[q, slots] = jnp.zeros((CL, HF), jnp.float32)

    loads[0].wait()
    loads[1].wait()
    for t in range(per_row):
        tcols[t] = jnp.transpose(tpos[:, t * CL : (t + 1) * CL])
    for t in range(clusters):
        srows[t] = spos[:, t * CL : (t + 1) * CL]
    spread = math.sqrt(math.log2(math.e))

    def basis(slot, carry):
        cell = cells_ref[0, 0, slot]
        target = lax.div(cell, clusters)
        near_source = cell - target * clusters
        across = tcols[target]
        along = srows[near_source]
        squared = jnp.zeros((CL, CL), jnp.float32)
        for component in range(3):
            difference = across[:, component : component + 1] - along[component : component + 1, :]
            squared = squared + difference * difference
        distance = jnp.sqrt(squared)
        target_ids = (row * per_row + target) * CL + lax.broadcasted_iota(jnp.int32, (CL, CL), 0)
        local_ids = lax.broadcasted_iota(jnp.int32, (CL, CL), 1)
        source_cluster = col * clusters + near_source
        real = jnp.where(slot < count_ref[0, 0], atoms_ref[source_cluster], 0)
        allowed = (
            (target_ids != source_cluster * CL + local_ids)
            & (local_ids < real)
            & (distance < CUTOFF)
        )
        envelope = jnp.where(allowed, envelope_of(squared), 0.0)
        reach = distance * ((NRBF - 1) / CUTOFF * spread)
        for k in range(NRBF):
            offset = reach - k * spread
            weights[slot, :, k * CL : (k + 1) * CL] = (
                jnp.exp2(-(offset * offset)) * envelope
            ).astype(jnp.bfloat16)
        return carry

    def scale(c, k):
        rows = source[c, k].astype(jnp.float32)
        for n in range(NRBF):
            for q in range(2):
                columns = slice(q * HF, (q + 1) * HF)
                scaled[q, c, n, k] = (filter_ref[n : n + 1, columns] * rows[:, columns]).astype(
                    jnp.bfloat16
                )

    early = slots * 2 // 3
    lax.fori_loop(0, early, basis, 0)
    for j in range(1, chips):
        row_copy(back(j), core, row_fwd.at[j], sibling).wait_recv()
        row_copy(back(j), core, row_fwd.at[j], sibling).start()

    def scale_own(j, carry):
        scale(back(j), core)
        return carry

    def scale_other(j, carry):
        row_copy(back(j), 1 - core, row_fwd.at[0], sibling).wait_recv()
        scale(back(j), 1 - core)
        return carry

    lax.fori_loop(0, chips, scale_own, 0)
    lax.fori_loop(early, slots, basis, 0)
    lax.fori_loop(0, chips, scale_other, 0)

    def ahead(way, d):
        return lax.rem(z + d, nz) if way == 0 else lax.rem(z + nz - d, nz)

    def behind(way, d):
        return ahead(1 - way, d)

    def both(q, *distances):
        return [(q, way, d) for d in distances for way in (ways if 0 < d < top else (0,))]

    odd = list(range(top - 1, 1, -2))
    even = list(range(top - 4, 1, -2))
    opening = (top, *odd, top - 2)
    crossing = [both(0, *opening), both(1, *opening)]
    work = both(0, top, *odd) + both(1, top, top - 1) + both(0, top - 2)
    work += both(1, *odd[1:], top - 2)
    for d in even:
        raw = (1,) if d == even[0] else ()
        crossing[1] += both(0, d, *raw) + both(1, d, *raw)
        work += both(0, d, *raw) + both(1, *raw, d)
    crossing[1] += both(0, 0) + both(1, 0)
    work += both(0, 0) + both(1, 0)
    order = [(way, d) for q, way, d in work if q == 0]
    last = {(way, d): last_of(ahead(way, d)) for way, d in order}

    def mine(place, which, q):
        return jobs[q, last[place], pl.ds(pl.multiple_of(which * HALF, HALF), HALF), :]

    def x_copy(t, q):
        return remote(xout.at[t, q], xin.at[t, q], x_send.at[t, q], x_recv.at[t, q], partner)

    for q in range(2):
        def job(slot, carry):
            cell = cells_ref[0, 0, slot]
            target = lax.div(cell, clusters)
            before = slots
            for other in range(slots - 1):
                before = jnp.where((targets[other] == target) & (other < slot), other, before)
            jobs[q, slot] = jobs[q, before] + jnp.dot(
                weights[slot],
                scaled[q, cell - target * clusters].reshape(NRBF * CL, HF),
                preferred_element_type=jnp.float32,
            )
            return carry

        lax.fori_loop(0, slots, job, 0)
        for p, way, d in crossing[q]:
            t = ahead(way, d)
            xout[t, p] = mine((way, d), 1 - h, p).astype(jnp.bfloat16)
            x_copy(t, p).start()

    def tip(q):
        return remote(tip_out.at[q], tip_in.at[q], tip_send.at[q], tip_recv.at[q], two[q])

    def near(way, d, q):
        i = (top - 1 - d) // 2
        return remote(
            zout.at[way, d - 1, q],
            near_in.at[way, i, q],
            near_send.at[way, i, q],
            near_recv.at[way, i, q],
            one[way],
        )

    def far(way, d, q):
        i = (top - 2 - d) // 2
        return remote(
            zout.at[way, d - 1, q],
            far_in.at[way, i, q],
            far_send.at[way, i, q],
            far_recv.at[way, i, q],
            two[way],
        )

    def come(way, d, q):
        near(way, d + 1, q).wait_recv()
        total = near_in[way, (top - 2 - d) // 2, q].astype(jnp.float32)
        if d + 2 == top:
            if way == q:
                tip(q).wait_recv()
                total = total + tip_in[q].astype(jnp.float32)
            return total
        far(way, d + 2, q).wait_recv()
        return total + far_in[way, (top - 4 - d) // 2, q].astype(jnp.float32)

    for q, way, d in work:
        t = ahead(way, d)
        x_copy(t, q).wait_recv()
        total = mine((way, d), h, q) + xin[t, q].astype(jnp.float32)
        if d == top:
            tip_out[q] = total.astype(jnp.bfloat16)
            tip(q).start()
        elif d % 2:
            zout[way, d - 1, q] = total.astype(jnp.bfloat16)
            near(way, d, q).start()
        elif d:
            zout[way, d - 1, q] = (total + come(way, d, q)).astype(jnp.bfloat16)
            far(way, d, q).start()
        else:
            message[:, q * HF : (q + 1) * HF] = (total + come(0, 0, q) + come(1, 0, q)).astype(
                jnp.bfloat16
            )

    loads[2].wait()
    loads[3].wait()
    hidden = jnp.dot(message[...], hw_ref[...], preferred_element_type=jnp.float32) + hb_ref[...]
    hidden = jnp.maximum(hidden, 0.0) + jnp.log1p(jnp.exp(-jnp.abs(hidden))) - math.log(2.0)
    result = (
        jnp.dot(hidden.astype(jnp.bfloat16), ow_ref[...], preferred_element_type=jnp.float32)
        + ob_ref[...]
    )
    atom = h * HALF + lax.broadcasted_iota(jnp.int32, (HALF, F), 0)
    valid = atoms_ref[row * per_row + z]
    out_v[z, h] = jnp.where(atom < valid, result, 0.0).astype(jnp.bfloat16)

    def g_near(way, e):
        ref = out_v.at[behind(way, e), h]
        i = e // 2
        return remote(ref, ref, gnear_send.at[way, i], gnear_recv.at[way, i], one[way])

    def g_far(way, e):
        i = e // 2
        if e + 2 == top:
            ref = out_v.at[behind(way, e), h, pl.ds(way * (HALF // 2), HALF // 2)]
        else:
            ref = out_v.at[behind(way, e), h]
        return remote(ref, ref, gfar_send.at[way, i], gfar_recv.at[way, i], two[way])

    def g_near_in(way, e):
        ref = out_v.at[behind(way, e + 1), h]
        i = e // 2
        remote(ref, ref, gnear_send.at[way, i], gnear_recv.at[way, i], one[way]).wait_recv()

    def g_far_in(way, e):
        i = e // 2
        if e + 2 == top:
            ref = out_v.at[behind(way, e + 2), h, pl.ds(way * (HALF // 2), HALF // 2)]
        else:
            ref = out_v.at[behind(way, e + 2), h]
        remote(ref, ref, gfar_send.at[way, i], gfar_recv.at[way, i], two[way]).wait_recv()

    def cross(t, which):
        ref = out_v.at[t, which]
        return remote(ref, ref, gx_send.at[t], gx_recv.at[t], partner)

    def store(t, which):
        return pltpu.make_async_copy(out_v.at[t, which], out_ref.at[t, which], out_sem.at[t, which])

    def keep(t):
        cross(t, h).start()
        store(t, h).start()

    for way in ways:
        g_far(way, 0).start()
    for way in ways:
        g_near(way, 0).start()
    keep(z)
    for e in range(2, top + 1, 2):
        for way in ways:
            g_far_in(way, e - 2)
            if e < top:
                g_far(way, e).start()
                g_near(way, e).start()
                keep(behind(way, e))
        if e == top:
            keep(behind(0, top))
        for way in ways:
            g_near_in(way, e - 2)
            keep(behind(way, e - 1))

    arrive = [z]
    for e in range(2, top, 2):
        arrive += [behind(way, e) for way in ways] + [behind(way, e - 1) for way in ways]
    arrive += [behind(0, top)] + [behind(way, top - 1) for way in ways]
    for t in arrive:
        cross(t, 1 - h).wait_recv()
        store(t, 1 - h).start()

    for j in range(1, chips):
        row_copy(chip, core, row_send.at[j], peers[j - 1]).wait_send()
    for j in range(chips):
        row_copy(back(j), core, row_fwd.at[j], sibling).wait_send()
    for w in ways:
        tip(w).wait_send()
        for q in range(2):
            for d in range(1, top):
                (near if d % 2 else far)(w, d, q).wait_send()
        for e in range(0, top, 2):
            g_near(w, e).wait_send()
            g_far(w, e).wait_send()

    def ended(t, carry):
        for which in range(2):
            x_copy(t, which).wait_send()
            store(t, which).wait()
        cross(t, h).wait_send()
        return carry

    lax.fori_loop(0, nz, ended, 0)


def local(
    n_row,
    n_col,
    features,
    positions,
    cluster_atoms,
    pair_cells,
    pair_count,
    project_weight,
    basis_filter,
    hidden_weight,
    hidden_bias,
    output_weight,
    output_bias,
):
    rows = features.shape[0]
    slots = pair_cells.shape[2]
    clusters = n_row * rows // CL
    nz = positions.shape[1] // CL // n_row
    top = nz // 2
    steps = top // 2
    bf16 = jnp.bfloat16
    dma = pltpu.SemaphoreType.DMA
    update = pl.pallas_call(
        functools.partial(kernel, n_row, nz, clusters, slots),
        out_shape=jax.ShapeDtypeStruct((nz, 2, HALF, F), bf16),
        in_specs=[
            vmem(),
            vmem(),
            smem(),
            smem(),
            smem(),
            hbm(),
            vmem(),
            hbm(),
            vmem(),
            hbm(),
            vmem(),
        ],
        out_specs=hbm(),
        scratch_shapes=[
            pltpu.VMEM((n_row // 2, 2, rows, F), bf16),
            pltpu.VMEM((8, nz * CL), jnp.float32),
            pltpu.VMEM((8, clusters * CL), jnp.float32),
            pltpu.VMEM((nz, CL, 8), jnp.float32),
            pltpu.VMEM((clusters, 8, CL), jnp.float32),
            pltpu.VMEM((F, F), bf16),
            pltpu.VMEM((F, F), bf16),
            pltpu.VMEM((slots, CL, NRBF * CL), bf16),
            pltpu.VMEM((2, clusters, NRBF, 2, HALF, HF), bf16),
            pltpu.VMEM((2, slots + 1, CL, HF), jnp.float32),
            pltpu.VMEM((nz, 2, HALF, HF), bf16),
            pltpu.VMEM((nz, 2, HALF, HF), bf16),
            pltpu.VMEM((2, HALF, HF), bf16),
            pltpu.VMEM((2, HALF, HF), bf16),
            pltpu.VMEM((2, steps - 1, 2, HALF, HF), bf16),
            pltpu.VMEM((2, steps, 2, HALF, HF), bf16),
            pltpu.VMEM((2, top - 1, 2, HALF, HF), bf16),
            pltpu.VMEM((HALF, F), bf16),
            pltpu.VMEM((nz, 2, HALF, F), bf16),
            dma((4,)),
            dma((n_row // 2,)),
            dma((n_row // 2, 2)),
            dma((n_row // 2,)),
            dma((nz, 2)),
            dma((nz, 2)),
            dma((2,)),
            dma((2,)),
            dma((2, steps - 1, 2)),
            dma((2, steps - 1, 2)),
            dma((2, steps, 2)),
            dma((2, steps, 2)),
            dma((nz,)),
            dma((nz,)),
            dma((2, steps)),
            dma((2, steps)),
            dma((2, steps)),
            dma((2, steps)),
            dma((nz, 2)),
        ],
        compiler_params=pltpu.CompilerParams(
            collective_id=0, has_side_effects=True, vmem_limit_bytes=VMEM_LIMIT
        ),
        name="interaction",
    )(
        features,
        project_weight,
        pair_cells,
        pair_count,
        cluster_atoms,
        positions,
        basis_filter,
        hidden_weight,
        hidden_bias.reshape(1, F),
        output_weight,
        output_bias.reshape(1, F),
    )
    return update.reshape(-1, F)


def solution(mesh):
    in_specs = (
        P(("col", "row"), None),
        P(),
        P(),
        P("row", "col", None),
        P("row", "col"),
        P(),
        P(),
        P(),
        P(),
        P(),
        P(),
    )
    out_specs = P("row", None)
    body = functools.partial(local, mesh.shape["row"], mesh.shape["col"])
    return jax.shard_map(body, mesh=mesh, in_specs=in_specs, out_specs=out_specs, check_vma=False)
```
